32 devices in a mesh: energy: 4 (over y, core), layer: 8 (over z, x).
Axes of the slice: x: 2, y: 2, z: 4, core: 2. Of those that a mesh axis runs over, the one named last changes fastest.
Arguments:
- correlations: bfloat16 [32, 8, 4, 256, 256], P(('energy', 'layer')), may hold values from -6 to 6
- retarded: bfloat16 [32, 8, 2, 256, 256], P(('energy', 'layer')), may hold values from -0.15625 to 0.15625
- coupling: bfloat16 [8, 256, 256], P('layer'), may hold values from -0.375 to 0.375
- phonon_shifts: int32 [4], replicated, may hold values from 1 to 4, as said below
- phonon_coupling: float32 [4], replicated, may hold values from 0.3 to 1.2
- layer_orbitals: int32 [8], P('layer'), may hold values from 128 to 256, as said below
Outputs:
- left_correlations: bfloat16 [32, 8, 4, 256, 256], P('energy', 'layer')
The draws below stay inside these ranges and needn't reach their ends.
Inputs may be any that keep to these rules, and one draw needn't show every extreme that they name: `phonon_shifts`: one of the offsets equals 4. `layer_orbitals`: some layer has all 256 orbitals live.
All inputs are finite; a program needn't handle non-finite values.
Results may differ from the reference program's by a relative error of at most 0.025.
Values may be sent and summed in bfloat16 or wider, within the bound.
A program may use at most 128 MiB of HBM per device.

```python
import math
import jax
import jax.numpy as jnp
from jax import lax

ORBITALS = 256
MODES = 4
SHIFT_MAX = 4
ENERGIES = 32
LAYERS = 8


def draw_phonon_shifts(key, part):
    first_key, second = jax.random.split(key)
    values = jax.random.randint(first_key, (MODES,), 1, SHIFT_MAX + 1)
    chosen = jax.random.randint(second, (), 0, MODES)
    return jnp.where(jnp.arange(MODES) == chosen, SHIFT_MAX, values).astype(jnp.int32)


def draw_layer_orbitals(key, part):
    first_key, second = jax.random.split(jax.random.fold_in(key, 7))
    values = jax.random.randint(first_key, (LAYERS,), ORBITALS // 2, ORBITALS + 1)
    chosen = jax.random.randint(second, (), 0, LAYERS)
    return jnp.where(jnp.arange(LAYERS) == chosen, ORBITALS, values).astype(jnp.int32)


def steps_of(rng, dims, shards, low, largest):
    def one(position, shards_of):
        heights = jax.random.uniform(jax.random.fold_in(jax.random.fold_in(rng, 6), position), (shards_of,), jnp.float32, low / len(shards), largest / len(shards))
        return jnp.repeat(jnp.exp(heights), dims[position] // shards_of).reshape((-1,) + (1,) * (len(dims) - position - 1))

    gain = one(*shards[0])
    for cut in shards[1:]:
        gain = gain * one(*cut)
    return gain


def noise(own_key, extent, scale, bound, cuts=(), held_as=jnp.bfloat16):
    values = scale * jax.random.normal(own_key, extent, jnp.float32)
    if cuts:
        values = values * steps_of(own_key, extent, cuts, -0.22, 0.18)
    return jnp.clip(values, -bound, bound).astype(held_as)


def setup_inputs(seed: int = 0) -> dict:
    key_list = jax.random.split(jax.random.key(seed), 7)
    correlations = noise(key_list[0], (ENERGIES, LAYERS, 4, ORBITALS, ORBITALS), 1.0, 6.0, ((0, 32),))
    retarded = noise(key_list[1], (ENERGIES, LAYERS, 2, ORBITALS, ORBITALS), (ORBITALS * 6) ** -0.5, 0.15625, ((0, 32),))
    coupling = noise(key_list[2], (LAYERS, ORBITALS, ORBITALS), ORBITALS ** -0.5, 0.375, ((0, 8),))
    phonon_shifts = draw_phonon_shifts(jax.random.fold_in(key_list[6], 71), 0)
    phonon_coupling = jnp.clip(jnp.exp(jax.random.uniform(key_list[4], (MODES,), jnp.float32, math.log(0.3), math.log(1.2))), 0.3, 1.2)
    layer_orbitals = draw_layer_orbitals(jax.random.fold_in(key_list[6], 71), 0)
    return dict(correlations=correlations, retarded=retarded, coupling=coupling, phonon_shifts=phonon_shifts, phonon_coupling=phonon_coupling, layer_orbitals=layer_orbitals)


bose_ratio = 0.5


def mode_weights(shift_value):
    occupation = 1.0 / (jnp.exp(bose_ratio * shift_value.astype(jnp.float32)) - 1.0)
    lower_weight = jnp.stack([occupation, occupation, occupation + 1.0, occupation + 1.0])
    upper_weight = jnp.stack([occupation + 1.0, occupation + 1.0, occupation, occupation])
    return lower_weight, upper_weight


def self_energy(piece_block, phonon_shifts, phonon_coupling, live_count):
    padded = jnp.pad(piece_block, ((SHIFT_MAX, SHIFT_MAX), (0, 0), (0, 0), (0, 0)))
    accumulated = jnp.zeros(piece_block.shape, jnp.float32)
    for mode_index in range(MODES):
        shift_value = phonon_shifts[mode_index]
        lower_weight, upper_weight = mode_weights(shift_value)
        lower_block = lax.dynamic_slice_in_dim(padded, (SHIFT_MAX - shift_value).astype(jnp.int32), ENERGIES, 0).astype(jnp.float32)
        upper_block = lax.dynamic_slice_in_dim(padded, (SHIFT_MAX + shift_value).astype(jnp.int32), ENERGIES, 0).astype(jnp.float32)
        accumulated = accumulated + phonon_coupling[mode_index] * (lower_weight[:, None, None] * lower_block + upper_weight[:, None, None] * upper_block)
    orbital_index = jnp.arange(ORBITALS, dtype=jnp.int32)
    live_mask = (orbital_index[:, None] < live_count) & (orbital_index[None, :] < live_count)
    return jnp.where(live_mask, accumulated, 0.0).astype(jnp.bfloat16)


def rounded(values):
    return lax.optimization_barrier(values.astype(jnp.bfloat16)).astype(jnp.float32)


def advance(previous, sigma_block, green_block, coupling_block):
    wide = jnp.float32
    coupling_wide = coupling_block.astype(wide)
    halfway = rounded(jnp.einsum('...kab,cb->...kac', previous.astype(wide), coupling_wide))
    spread = jnp.einsum('ab,...kbc->...kac', coupling_wide, halfway)
    source = rounded(sigma_block.astype(wide) + spread)
    green_real = green_block[..., 0, :, :].astype(wide)
    green_imag = green_block[..., 1, :, :].astype(wide)
    source_real = source[..., 0::2, :, :]
    source_imag = source[..., 1::2, :, :]
    inner_real = rounded(jnp.einsum('...ab,...kbc->...kac', green_real, source_real) - jnp.einsum('...ab,...kbc->...kac', green_imag, source_imag))
    inner_imag = rounded(jnp.einsum('...ab,...kbc->...kac', green_real, source_imag) + jnp.einsum('...ab,...kbc->...kac', green_imag, source_real))
    outer_real = jnp.einsum('...kab,...cb->...kac', inner_real, green_real) + jnp.einsum('...kab,...cb->...kac', inner_imag, green_imag)
    outer_imag = jnp.einsum('...kab,...cb->...kac', inner_imag, green_real) - jnp.einsum('...kab,...cb->...kac', inner_real, green_imag)
    stacked = jnp.stack([outer_real, outer_imag], axis=-3)
    return stacked.reshape(stacked.shape[:-4] + (4, ORBITALS, ORBITALS)).astype(jnp.bfloat16)


def reference(correlations, retarded, coupling, phonon_shifts, phonon_coupling, layer_orbitals):
    def layer_step(previous, layer_index):
        piece_block = lax.dynamic_index_in_dim(correlations, layer_index, 1, keepdims=False)
        live_count = lax.dynamic_index_in_dim(layer_orbitals, layer_index, 0, keepdims=False)
        sigma_block = self_energy(piece_block, phonon_shifts, phonon_coupling, live_count)
        green_block = lax.dynamic_index_in_dim(retarded, layer_index, 1, keepdims=False)
        coupling_block = lax.dynamic_index_in_dim(coupling, layer_index, 0, keepdims=False)
        current = advance(previous, sigma_block, green_block, coupling_block)
        return current, current

    lead_block = correlations[:, 0]
    _, layers = lax.scan(layer_step, lead_block, jnp.arange(LAYERS, dtype=jnp.int32))
    return jnp.moveaxis(layers, 0, 1)
```

```python
import functools

import jax
import jax.numpy as jnp
from jax import lax
from jax.experimental import pallas as pl
from jax.experimental.pallas import tpu as pltpu
from jax.sharding import PartitionSpec as P

SHIFT_MAX = 4
MESH = pl.DeviceIdType.MESH
ROWS = 32

bose_ratio = 0.5


def tap_weights(phonon_shifts, phonon_coupling):
    occupation = 1.0 / (jnp.exp(bose_ratio * phonon_shifts.astype(jnp.float32)) - 1.0)
    distance = jnp.arange(1, SHIFT_MAX + 1, dtype=jnp.int32)
    here = phonon_shifts[None, :] == distance[:, None]
    absorb = jnp.sum(jnp.where(here, phonon_coupling * occupation, 0.0), axis=1)
    emit = jnp.sum(jnp.where(here, phonon_coupling * (occupation + 1.0), 0.0), axis=1)
    return jnp.concatenate([absorb, emit])


def dot(a, b):
    return lax.dot_general(a, b, (((1,), (0,)), ((), ())), preferred_element_type=jnp.float32)


def dot_t(a, b):
    return lax.dot_general(a, b, (((1,), (1,)), ((), ())), preferred_element_type=jnp.float32)


def kernel(
    groups, lines, orbitals,
    weights, corr, ret, coupling, live, out,
    buf, green, volt, alive, sigma, xin, xout,
    own_sem, line_s, line_r, part_s, part_r, halo_s, halo_r,
    ret_own, ret_s, ret_r, side_sem, chain_s, chain_r, out_sem, out_s, out_r,
):
    energies = 2 * lines
    e = lax.axis_index("energy")
    index = lax.axis_index("layer")
    p = index // 2
    q = lax.rem(index, 2)
    partner = {"layer": 2 * p + (1 - q)}
    half = jnp.bfloat16

    def peer(d):
        return lax.rem(p + d, lines)

    def source(d):
        return lax.rem(p + lines - d, lines)

    barrier = pltpu.get_barrier_semaphore()
    for d in range(1, lines):
        pl.semaphore_signal(barrier, inc=1, device_id={"layer": 2 * peer(d) + q}, device_id_type=MESH)
    pl.semaphore_signal(barrier, inc=1, device_id=partner, device_id_type=MESH)

    @pl.when(e > 0)
    def _():
        pl.semaphore_signal(barrier, inc=1, device_id={"energy": e - 1}, device_id_type=MESH)

    @pl.when(e < groups - 1)
    def _():
        pl.semaphore_signal(barrier, inc=1, device_id={"energy": e + 1}, device_id_type=MESH)

    beside = (e > 0).astype(jnp.int32) + (e < groups - 1).astype(jnp.int32)
    pl.semaphore_wait(barrier, lines + beside)

    def slot_of(line, parity):
        return SHIFT_MAX + 2 * line + parity

    def own_copy(k):
        c, a = divmod(k, 2)
        return pltpu.make_async_copy(
            corr.at[0, 2 * p + a, pl.ds(2 * c, 2)], buf.at[k, slot_of(p, q)], own_sem.at[k]
        )

    def line_copy(k, d, arriving=False):
        c, a = divmod(k, 2)
        line = source(d) if arriving else p
        return pltpu.make_async_remote_copy(
            src_ref=corr.at[0, 2 * peer(d) + a, pl.ds(2 * c, 2)],
            dst_ref=buf.at[k, slot_of(line, q)],
            send_sem=line_s.at[k, d], recv_sem=line_r.at[k, d],
            device_id={"layer": 2 * peer(d) + q}, device_id_type=MESH,
        )

    def part_copy(k, d, arriving=False):
        slot = slot_of(source(d), 1 - q if arriving else q)
        return pltpu.make_async_remote_copy(
            src_ref=buf.at[k, slot], dst_ref=buf.at[k, slot],
            send_sem=part_s.at[k, d], recv_sem=part_r.at[k, d],
            device_id=partner, device_id_type=MESH,
        )

    def halo_copy(k, side):
        first = SHIFT_MAX if side == 0 else energies
        landing = SHIFT_MAX + energies if side == 0 else 0
        return pltpu.make_async_remote_copy(
            src_ref=buf.at[k, pl.ds(first, SHIFT_MAX)],
            dst_ref=buf.at[k, pl.ds(landing, SHIFT_MAX)],
            send_sem=halo_s.at[k, side], recv_sem=halo_r.at[k, side],
            device_id={"energy": e - 1 if side == 0 else e + 1}, device_id_type=MESH,
        )

    def ret_own_copy():
        return pltpu.make_async_copy(ret.at[0, pl.ds(2 * p, 2)], green.at[p], ret_own)

    def ret_copy(d, arriving=False):
        line = source(d) if arriving else p
        return pltpu.make_async_remote_copy(
            src_ref=ret.at[0, pl.ds(2 * peer(d), 2)], dst_ref=green.at[line],
            send_sem=ret_s.at[d], recv_sem=ret_r.at[d],
            device_id={"layer": 2 * peer(d) + q}, device_id_type=MESH,
        )

    def side_copies(arriving=False):
        at = 1 - q if arriving else q
        return (
            pltpu.make_async_remote_copy(
                src_ref=coupling.at[0], dst_ref=volt.at[at],
                send_sem=side_sem.at[0], recv_sem=side_sem.at[1],
                device_id=partner, device_id_type=MESH,
            ),
            pltpu.make_async_remote_copy(
                src_ref=live, dst_ref=alive.at[at],
                send_sem=side_sem.at[2], recv_sem=side_sem.at[3],
                device_id=partner, device_id_type=MESH,
            ),
        )

    def side_own():
        return (
            pltpu.make_async_copy(coupling.at[0], volt.at[q], side_sem.at[4]),
            pltpu.make_async_copy(live, alive.at[q], side_sem.at[5]),
        )

    def chain_copy(c, i):
        return pltpu.make_async_remote_copy(
            src_ref=xout.at[c, 1, i], dst_ref=xin.at[c, i],
            send_sem=chain_s.at[c, i], recv_sem=chain_r.at[c, i],
            device_id={"layer": lax.rem(index + 2, 2 * lines)}, device_id_type=MESH,
        )

    def out_own(c, i):
        return pltpu.make_async_copy(
            xout.at[c, q, i], out.at[2 * i + q, 0, pl.ds(2 * c, 2)], out_sem.at[c, i]
        )

    def out_copy(c, i, arriving=False):
        parity = 1 - q if arriving else q
        return pltpu.make_async_remote_copy(
            src_ref=xout.at[c, 1 - q, i], dst_ref=out.at[2 * i + parity, 0, pl.ds(2 * c, 2)],
            send_sem=out_s.at[c, i], recv_sem=out_r.at[c, i],
            device_id=partner, device_id_type=MESH,
        )

    def start_line(k):
        own_copy(k).start()
        for d in range(1, lines):
            line_copy(k, d).start()

    def pass_on(k):
        for d in range(lines):
            if d == 0:
                own_copy(k).wait()
            else:
                line_copy(k, d, True).wait_recv()
            part_copy(k, d).start()

    def start_halo(k):
        for d in range(lines):
            part_copy(k, d, True).wait_recv()

        @pl.when(e > 0)
        def _():
            halo_copy(k, 0).start()

        @pl.when(e < groups - 1)
        def _():
            halo_copy(k, 1).start()

    def self_energy(k):
        c, a = divmod(k, 2)

        @pl.when(e < groups - 1)
        def _():
            halo_copy(k, 0).wait_recv()

        @pl.when(e > 0)
        def _():
            halo_copy(k, 1).wait_recv()

        absorb = [weights[d] for d in range(SHIFT_MAX)]
        emit = [weights[SHIFT_MAX + d] for d in range(SHIFT_MAX)]
        below, above = (absorb, emit) if c == 0 else (emit, absorb)
        count = alive[a, 0:1, :]
        column = lax.broadcasted_iota(jnp.int32, (ROWS, orbitals), 1)
        row = lax.broadcasted_iota(jnp.int32, (ROWS, orbitals), 0)
        tiles = orbitals // ROWS

        def one(step, carry):
            i = step // (2 * tiles)
            component = lax.rem(step // tiles, 2)
            base = pl.multiple_of(lax.rem(step, tiles) * ROWS, ROWS)
            here = slot_of(i, q)
            total = jnp.zeros((ROWS, orbitals), jnp.float32)
            for d in range(SHIFT_MAX):
                low = buf[k, here - d - 1, component, pl.ds(base, ROWS), :].astype(jnp.float32)
                high = buf[k, here + d + 1, component, pl.ds(base, ROWS), :].astype(jnp.float32)
                total = total + (below[d] * low + above[d] * high)
            keep = (row + base < count) & (column < count)
            sigma[k, i, component, pl.ds(base, ROWS), :] = jnp.where(keep, total, 0.0).astype(half)
            return carry

        lax.fori_loop(0, lines * 2 * tiles, one, 0)

    def advance(c, a, i, previous):
        k = 2 * c + a
        v = volt[a]
        g_real = green[i, a, 0]
        g_imag = green[i, a, 1]
        halfway = [dot_t(previous[n], v).astype(half) for n in range(2)]
        src = [
            (sigma[k, i, n].astype(jnp.float32) + dot(v, halfway[n])).astype(half) for n in range(2)
        ]
        inner_real = (dot(g_real, src[0]) - dot(g_imag, src[1])).astype(half)
        inner_imag = (dot(g_real, src[1]) + dot(g_imag, src[0])).astype(half)
        xout[c, a, i, 0] = (dot_t(inner_real, g_real) + dot_t(inner_imag, g_imag)).astype(half)
        xout[c, a, i, 1] = (dot_t(inner_imag, g_real) - dot_t(inner_real, g_imag)).astype(half)

    def sweep(c, first, last):
        def one(i, carry):
            @pl.when(p == 0)
            def _():
                xin[c, i] = buf[2 * c, slot_of(i, q)]

            @pl.when(p > 0)
            def _():
                chain_copy(c, i).wait_recv()

            advance(c, 0, i, xin.at[c, i])
            advance(c, 1, i, xout.at[c, 0, i])

            @pl.when(p < lines - 1)
            def _():
                chain_copy(c, i).start()

            out_copy(c, i).start()
            out_own(c, i).start()
            return carry

        lax.fori_loop(first, last, one, 0)

    start_line(0)
    for copy in side_own() + side_copies():
        copy.start()
    start_line(1)

    for at, edge in ((0, 0), (SHIFT_MAX + energies, groups - 1)):
        @pl.when(e == edge)
        def _(at=at):
            def clear(step, carry):
                k = step // SHIFT_MAX
                slot = at + lax.rem(step, SHIFT_MAX)
                buf[k, slot] = jnp.zeros(buf.shape[2:], half)
                return carry

            lax.fori_loop(0, 4 * SHIFT_MAX, clear, 0)

    pass_on(0)
    ret_own_copy().start()
    for d in range(1, lines):
        ret_copy(d).start()
    pass_on(1)
    start_line(2)
    start_halo(0)
    start_halo(1)
    for copy in side_own():
        copy.wait()
    for copy in side_copies(True):
        copy.wait_recv()
    self_energy(0)
    self_energy(1)
    ret_own_copy().wait()
    for d in range(1, lines):
        ret_copy(d, True).wait_recv()
    start_line(3)
    middle = lines // 2
    sweep(0, 0, middle)
    pass_on(2)
    sweep(0, middle, lines)
    start_halo(2)
    pass_on(3)
    self_energy(2)
    start_halo(3)
    self_energy(3)
    sweep(1, 0, lines)

    for copy in side_copies():
        copy.wait_send()
    for d in range(1, lines):
        ret_copy(d).wait_send()
        for k in range(4):
            line_copy(k, d).wait_send()
    for k in range(4):
        for d in range(lines):
            part_copy(k, d).wait_send()

        @pl.when(e > 0)
        def _(k=k):
            halo_copy(k, 0).wait_send()

        @pl.when(e < groups - 1)
        def _(k=k):
            halo_copy(k, 1).wait_send()

    for c in range(2):
        def finish(i, carry, c=c):
            @pl.when(p < lines - 1)
            def _():
                chain_copy(c, i).wait_send()

            out_own(c, i).wait()
            out_copy(c, i).wait_send()
            out_copy(c, i, True).wait_recv()
            return carry

        lax.fori_loop(0, lines, finish, 0)


def body(correlations, retarded, coupling, phonon_shifts, phonon_coupling, layer_orbitals):
    groups = lax.axis_size("energy")
    energies = lax.axis_size("layer")
    lines = energies // 2
    orbitals = correlations.shape[-1]
    weights = tap_weights(phonon_shifts, phonon_coupling)
    live = jnp.broadcast_to(layer_orbitals[0], (8, orbitals)).astype(jnp.int32)
    block = (2, orbitals, orbitals)
    low = jnp.bfloat16
    shapes = [
        (4, energies + 2 * SHIFT_MAX) + block,
        (lines, 2) + block,
        (2, orbitals, orbitals),
        None,
        (4, lines) + block,
        (2, lines) + block,
        (2, 2, lines) + block,
    ]
    scratch = [
        pltpu.VMEM((2, 8, orbitals), jnp.int32) if shape is None else pltpu.VMEM(shape, low)
        for shape in shapes
    ]
    blocks = 4 * (energies + 2 * SHIFT_MAX) + 2 * lines + 1 + 4 * lines + 2 * lines + 4 * lines
    dma = pltpu.SemaphoreType.DMA
    semaphores = [
        dma((4,)), dma((4, lines)), dma((4, lines)), dma((4, lines)), dma((4, lines)),
        dma((4, 2)), dma((4, 2)),
        dma(()), dma((lines,)), dma((lines,)), dma((6,)),
        dma((2, lines)), dma((2, lines)), dma((2, lines)), dma((2, lines)), dma((2, lines)),
    ]
    anywhere = pl.BlockSpec(memory_space=pl.ANY)
    return pl.pallas_call(
        functools.partial(kernel, groups, lines, orbitals),
        out_shape=jax.ShapeDtypeStruct((energies, 1, 4, orbitals, orbitals), low),
        in_specs=[pl.BlockSpec(memory_space=pltpu.SMEM)] + [anywhere] * 4,
        out_specs=anywhere,
        scratch_shapes=scratch + semaphores,
        compiler_params=pltpu.CompilerParams(
            collective_id=0, has_side_effects=True,
            vmem_limit_bytes=blocks * 4 * orbitals * orbitals + (8 << 20),
        ),
        cost_estimate=pl.CostEstimate(
            flops=lines * 4 * 12 * 2 * orbitals**3, bytes_accessed=12 << 20, transcendentals=0
        ),
    )(weights, correlations, retarded, coupling, live)


def solution(mesh):
    return jax.shard_map(
        body,
        mesh=mesh,
        in_specs=(
            P(("energy", "layer"), None, None, None, None),
            P(("energy", "layer"), None, None, None, None),
            P("layer", None, None),
            P(),
            P(),
            P("layer"),
        ),
        out_specs=P("energy", "layer", None, None, None),
        check_vma=False,
    )
```

```python
import functools
import math

import jax
import jax.numpy as jnp
from jax import lax
from jax.experimental import pallas as pl
from jax.experimental.pallas import tpu as pltpu
from jax.sharding import PartitionSpec as P

SHIFT_MAX = 4
MESH = pl.DeviceIdType.MESH
ROWS = 32

bose_ratio = 0.5


def tap_weights(shifts, strengths):
    absorb, emit = [], []
    for distance in range(1, SHIFT_MAX + 1):
        strength = jnp.float32(0)
        for mode in range(shifts.shape[0]):
            strength += jnp.where(shifts[mode] == distance, strengths[mode], jnp.float32(0))
        occupation = 1.0 / math.expm1(bose_ratio * distance)
        absorb.append(strength * jnp.float32(occupation))
        emit.append(strength * jnp.float32(occupation + 1.0))
    return absorb, emit


def dot(a, b):
    return lax.dot_general(a, b, (((1,), (0,)), ((), ())), preferred_element_type=jnp.float32)


def dot_t(a, b):
    return lax.dot_general(a, b, (((1,), (1,)), ((), ())), preferred_element_type=jnp.float32)


def kernel(
    groups, lines, orbitals,
    shifts, strengths, orbital_count, corr, ret, coupling, out,
    buf, green, volt, alive, sigma, xin, xout,
    own_sem, line_s, line_r, part_s, part_r, halo_s, halo_r,
    ret_own, ret_s, ret_r, side_sem, chain_s, chain_r, out_sem, out_s, out_r,
):
    energies = 2 * lines
    e = lax.axis_index("energy")
    index = lax.axis_index("layer")
    p = index // 2
    q = lax.rem(index, 2)
    partner = {"layer": 2 * p + (1 - q)}
    half = jnp.bfloat16

    def peer(d):
        return lax.rem(p + d, lines)

    def source(d):
        return lax.rem(p + lines - d, lines)

    barrier = pltpu.get_barrier_semaphore()
    for d in range(1, lines):
        pl.semaphore_signal(barrier, inc=1, device_id={"layer": 2 * peer(d) + q}, device_id_type=MESH)
    pl.semaphore_signal(barrier, inc=1, device_id=partner, device_id_type=MESH)

    @pl.when(e > 0)
    def _():
        pl.semaphore_signal(barrier, inc=1, device_id={"energy": e - 1}, device_id_type=MESH)

    @pl.when(e < groups - 1)
    def _():
        pl.semaphore_signal(barrier, inc=1, device_id={"energy": e + 1}, device_id_type=MESH)

    beside = (e > 0).astype(jnp.int32) + (e < groups - 1).astype(jnp.int32)
    pl.semaphore_wait(barrier, lines + beside)

    def slot_of(line, parity):
        return SHIFT_MAX + 2 * line + parity

    def own_copy(k):
        c, a = divmod(k, 2)
        return pltpu.make_async_copy(
            corr.at[0, 2 * p + a, pl.ds(2 * c, 2)], buf.at[k, slot_of(p, q)], own_sem.at[k]
        )

    def line_copy(k, d, arriving=False):
        c, a = divmod(k, 2)
        line = source(d) if arriving else p
        return pltpu.make_async_remote_copy(
            src_ref=corr.at[0, 2 * peer(d) + a, pl.ds(2 * c, 2)],
            dst_ref=buf.at[k, slot_of(line, q)],
            send_sem=line_s.at[k, d], recv_sem=line_r.at[k, d],
            device_id={"layer": 2 * peer(d) + q}, device_id_type=MESH,
        )

    def part_copy(k, d, arriving=False):
        slot = slot_of(source(d), 1 - q if arriving else q)
        return pltpu.make_async_remote_copy(
            src_ref=buf.at[k, slot], dst_ref=buf.at[k, slot],
            send_sem=part_s.at[k, d], recv_sem=part_r.at[k, d],
            device_id=partner, device_id_type=MESH,
        )

    def halo_copy(k, side):
        first = SHIFT_MAX if side == 0 else energies
        landing = SHIFT_MAX + energies if side == 0 else 0
        return pltpu.make_async_remote_copy(
            src_ref=buf.at[k, pl.ds(first, SHIFT_MAX)],
            dst_ref=buf.at[k, pl.ds(landing, SHIFT_MAX)],
            send_sem=halo_s.at[k, side], recv_sem=halo_r.at[k, side],
            device_id={"energy": e - 1 if side == 0 else e + 1}, device_id_type=MESH,
        )

    def ret_own_copy():
        return pltpu.make_async_copy(ret.at[0, pl.ds(2 * p, 2)], green.at[p], ret_own)

    def ret_copy(d, arriving=False):
        line = source(d) if arriving else p
        return pltpu.make_async_remote_copy(
            src_ref=ret.at[0, pl.ds(2 * peer(d), 2)], dst_ref=green.at[line],
            send_sem=ret_s.at[d], recv_sem=ret_r.at[d],
            device_id={"layer": 2 * peer(d) + q}, device_id_type=MESH,
        )

    def side_copies(arriving=False):
        at = 1 - q if arriving else q
        return (
            pltpu.make_async_remote_copy(
                src_ref=coupling.at[0], dst_ref=volt.at[at],
                send_sem=side_sem.at[0], recv_sem=side_sem.at[1],
                device_id=partner, device_id_type=MESH,
            ),
            pltpu.make_async_remote_copy(
                src_ref=alive.at[at], dst_ref=alive.at[at],
                send_sem=side_sem.at[2], recv_sem=side_sem.at[3],
                device_id=partner, device_id_type=MESH,
            ),
        )

    def side_own():
        return pltpu.make_async_copy(coupling.at[0], volt.at[q], side_sem.at[4])

    def chain_copy(c, i):
        return pltpu.make_async_remote_copy(
            src_ref=xout.at[c, 1, i], dst_ref=xin.at[c, i],
            send_sem=chain_s.at[c, i], recv_sem=chain_r.at[c, i],
            device_id={"layer": lax.rem(index + 2, 2 * lines)}, device_id_type=MESH,
        )

    def out_own(c, i):
        return pltpu.make_async_copy(
            xout.at[c, q, i], out.at[2 * i + q, 0, pl.ds(2 * c, 2)], out_sem.at[c, i]
        )

    def out_copy(c, i, arriving=False):
        parity = 1 - q if arriving else q
        return pltpu.make_async_remote_copy(
            src_ref=xout.at[c, 1 - q, i], dst_ref=out.at[2 * i + parity, 0, pl.ds(2 * c, 2)],
            send_sem=out_s.at[c, i], recv_sem=out_r.at[c, i],
            device_id=partner, device_id_type=MESH,
        )

    def start_line(k):
        own_copy(k).start()
        for d in range(1, lines):
            line_copy(k, d).start()

    def arrival(t):
        line = jnp.where(p < lines // 2, t, lines - 1 - t)
        return line, lax.rem(p + lines - line, lines)

    def pass_on(k, meanwhile=None):
        own_copy(k).wait()
        part_copy(k, 0).start()
        for t in range(lines):
            line, d = arrival(t)

            @pl.when(line != p)
            def _():
                line_copy(k, d, True).wait_recv()
                part_copy(k, d).start()

            if t == lines // 2 and meanwhile is not None:
                meanwhile()

    def start_halo(k):
        for d in range(lines):
            part_copy(k, d, True).wait_recv()

        @pl.when(e > 0)
        def _():
            halo_copy(k, 0).start()

        @pl.when(e < groups - 1)
        def _():
            halo_copy(k, 1).start()

    def self_energy(k):
        c, a = divmod(k, 2)

        @pl.when(e < groups - 1)
        def _():
            halo_copy(k, 0).wait_recv()

        @pl.when(e > 0)
        def _():
            halo_copy(k, 1).wait_recv()

        absorb, emit = tap_weights(shifts, strengths)
        below, above = (absorb, emit) if c == 0 else (emit, absorb)
        count = alive[a, 0:1, :]
        column = lax.broadcasted_iota(jnp.int32, (ROWS, orbitals), 1)
        row = lax.broadcasted_iota(jnp.int32, (ROWS, orbitals), 0)
        tiles = orbitals // ROWS

        def one(step, carry):
            i = step // (2 * tiles)
            component = lax.rem(step // tiles, 2)
            base = pl.multiple_of(lax.rem(step, tiles) * ROWS, ROWS)
            here = slot_of(i, q)
            total = jnp.zeros((ROWS, orbitals), jnp.float32)
            for d in range(SHIFT_MAX):
                low = buf[k, here - d - 1, component, pl.ds(base, ROWS), :].astype(jnp.float32)
                high = buf[k, here + d + 1, component, pl.ds(base, ROWS), :].astype(jnp.float32)
                total = total + (below[d] * low + above[d] * high)
            keep = (row + base < count) & (column < count)
            sigma[k, i, component, pl.ds(base, ROWS), :] = jnp.where(keep, total, 0.0).astype(half)
            return carry

        lax.fori_loop(0, lines * 2 * tiles, one, 0)

    def advance(c, a, i, previous):
        k = 2 * c + a
        v = volt[a]
        g_real = green[i, a, 0]
        g_imag = green[i, a, 1]
        halfway = [dot_t(previous[n], v).astype(half) for n in range(2)]
        src = [
            (sigma[k, i, n].astype(jnp.float32) + dot(v, halfway[n])).astype(half) for n in range(2)
        ]
        inner_real = (dot(g_real, src[0]) - dot(g_imag, src[1])).astype(half)
        inner_imag = (dot(g_real, src[1]) + dot(g_imag, src[0])).astype(half)
        xout[c, a, i, 0] = (dot_t(inner_real, g_real) + dot_t(inner_imag, g_imag)).astype(half)
        xout[c, a, i, 1] = (dot_t(inner_imag, g_real) - dot_t(inner_real, g_imag)).astype(half)

    def sweep(c, first, last):
        def one(i, carry):
            @pl.when(p == 0)
            def _():
                xin[c, i] = buf[2 * c, slot_of(i, q)]

            @pl.when(p > 0)
            def _():
                chain_copy(c, i).wait_recv()

            advance(c, 0, i, xin.at[c, i])
            advance(c, 1, i, xout.at[c, 0, i])

            @pl.when(p < lines - 1)
            def _():
                @pl.when(i > 0)
                def _():
                    chain_copy(c, i - 1).wait_send()

                chain_copy(c, i).start()

            out_copy(c, i).start()
            out_own(c, i).start()
            return carry

        lax.fori_loop(first, last, one, 0)

    start_line(0)
    alive[q] = jnp.full(alive.shape[1:], orbital_count[0], jnp.int32)
    side_own().start()
    for copy in side_copies():
        copy.start()

    for at, edge in ((0, 0), (SHIFT_MAX + energies, groups - 1)):
        @pl.when(e == edge)
        def _(at=at):
            def clear(step, carry):
                k = step // SHIFT_MAX
                slot = at + lax.rem(step, SHIFT_MAX)
                buf[k, slot] = jnp.zeros(buf.shape[2:], half)
                return carry

            lax.fori_loop(0, 4 * SHIFT_MAX, clear, 0)

    def start_ret():
        ret_own_copy().start()
        for d in range(1, lines):
            ret_copy(d).start()

    pass_on(0, lambda: start_line(1))
    pass_on(1, start_ret)
    start_halo(0)
    start_line(2)
    start_halo(1)
    side_own().wait()
    for copy in side_copies(True):
        copy.wait_recv()
    self_energy(0)
    self_energy(1)
    ret_own_copy().wait()
    for d in range(1, lines):
        ret_copy(d, True).wait_recv()
    start_line(3)
    sweep(0, 0, lines)
    pass_on(2)
    start_halo(2)
    pass_on(3)
    self_energy(2)
    start_halo(3)
    self_energy(3)
    sweep(1, 0, lines)

    for copy in side_copies():
        copy.wait_send()
    for d in range(1, lines):
        ret_copy(d).wait_send()
        for k in range(4):
            line_copy(k, d).wait_send()
    for k in range(4):
        for d in range(lines):
            part_copy(k, d).wait_send()

        @pl.when(e > 0)
        def _(k=k):
            halo_copy(k, 0).wait_send()

        @pl.when(e < groups - 1)
        def _(k=k):
            halo_copy(k, 1).wait_send()

    for c in range(2):
        def finish(i, carry, c=c):
            @pl.when((p < lines - 1) & (i == lines - 1))
            def _():
                chain_copy(c, i).wait_send()

            out_own(c, i).wait()
            out_copy(c, i).wait_send()
            out_copy(c, i, True).wait_recv()
            return carry

        lax.fori_loop(0, lines, finish, 0)


def body(correlations, retarded, coupling, phonon_shifts, phonon_coupling, layer_orbitals):
    groups = lax.axis_size("energy")
    energies = lax.axis_size("layer")
    lines = energies // 2
    orbitals = correlations.shape[-1]
    block = (2, orbitals, orbitals)
    low = jnp.bfloat16
    shapes = [
        (4, energies + 2 * SHIFT_MAX) + block,
        (lines, 2) + block,
        (2, orbitals, orbitals),
        None,
        (4, lines) + block,
        (2, lines) + block,
        (2, 2, lines) + block,
    ]
    scratch = [
        pltpu.VMEM((2, 8, orbitals), jnp.int32) if shape is None else pltpu.VMEM(shape, low)
        for shape in shapes
    ]
    dma = pltpu.SemaphoreType.DMA
    semaphores = [
        dma((4,)), dma((4, lines)), dma((4, lines)), dma((4, lines)), dma((4, lines)),
        dma((4, 2)), dma((4, 2)),
        dma(()), dma((lines,)), dma((lines,)), dma((6,)),
        dma((2, lines)), dma((2, lines)), dma((2, lines)), dma((2, lines)), dma((2, lines)),
    ]
    anywhere = pl.BlockSpec(memory_space=pl.ANY)
    return pl.pallas_call(
        functools.partial(kernel, groups, lines, orbitals),
        out_shape=jax.ShapeDtypeStruct((energies, 1, 4, orbitals, orbitals), low),
        in_specs=[pl.BlockSpec(memory_space=pltpu.SMEM)] * 3 + [anywhere] * 3,
        out_specs=anywhere,
        scratch_shapes=scratch + semaphores,
        compiler_params=pltpu.CompilerParams(
            collective_id=0, has_side_effects=True,
            vmem_limit_bytes=60 << 20,
        ),
        cost_estimate=pl.CostEstimate(
            flops=lines * 4 * 12 * 2 * orbitals**3, bytes_accessed=12 << 20, transcendentals=0
        ),
    )(phonon_shifts, phonon_coupling, layer_orbitals, correlations, retarded, coupling)


def solution(mesh):
    return jax.shard_map(
        body,
        mesh=mesh,
        in_specs=(
            P(("energy", "layer"), None, None, None, None),
            P(("energy", "layer"), None, None, None, None),
            P("layer", None, None),
            P(),
            P(),
            P("layer"),
        ),
        out_specs=P("energy", "layer", None, None, None),
        check_vma=False,
    )
```

```python
import functools
import math

import jax
import jax.numpy as jnp
from jax import lax
from jax.experimental import pallas as pl
from jax.experimental.pallas import tpu as pltpu
from jax.sharding import PartitionSpec as P

SHIFT_MAX = 4
MESH = pl.DeviceIdType.MESH
ROWS = 32

bose_ratio = 0.5


def tap_weights(shifts, strengths):
    absorb, emit = [], []
    for distance in range(1, SHIFT_MAX + 1):
        strength = jnp.float32(0)
        for mode in range(shifts.shape[0]):
            strength += jnp.where(shifts[mode] == distance, strengths[mode], jnp.float32(0))
        occupation = 1.0 / math.expm1(bose_ratio * distance)
        absorb.append(strength * jnp.float32(occupation))
        emit.append(strength * jnp.float32(occupation + 1.0))
    return absorb, emit


def dot(a, b):
    return lax.dot_general(a, b, (((1,), (0,)), ((), ())), preferred_element_type=jnp.float32)


def dot_t(a, b):
    return lax.dot_general(a, b, (((1,), (1,)), ((), ())), preferred_element_type=jnp.float32)


def kernel(
    groups, lines, orbitals,
    shifts, strengths, orbital_count, corr, ret, coupling, out,
    buf, green, volt, alive, sigma, xin, xout,
    own_sem, line_s, line_r, part_s, part_r, halo_s, halo_r,
    ret_own, ret_s, ret_r, side_sem, chain_s, chain_r, out_sem, out_s, out_r,
):
    energies = 2 * lines
    e = lax.axis_index("energy")
    index = lax.axis_index("layer")
    p = index // 2
    q = lax.rem(index, 2)
    partner = {"layer": 2 * p + (1 - q)}
    half = jnp.bfloat16

    def peer(d):
        return lax.rem(p + d, lines)

    def source(d):
        return lax.rem(p + lines - d, lines)

    barrier = pltpu.get_barrier_semaphore()
    for d in range(1, lines):
        pl.semaphore_signal(barrier, inc=1, device_id={"layer": 2 * peer(d) + q}, device_id_type=MESH)
    pl.semaphore_signal(barrier, inc=1, device_id=partner, device_id_type=MESH)

    @pl.when(e > 0)
    def _():
        pl.semaphore_signal(barrier, inc=1, device_id={"energy": e - 1}, device_id_type=MESH)

    @pl.when(e < groups - 1)
    def _():
        pl.semaphore_signal(barrier, inc=1, device_id={"energy": e + 1}, device_id_type=MESH)

    beside = (e > 0).astype(jnp.int32) + (e < groups - 1).astype(jnp.int32)
    pl.semaphore_wait(barrier, lines + beside)

    def slot_of(line, parity):
        return SHIFT_MAX + 2 * line + parity

    def own_copy(k):
        c, a = divmod(k, 2)
        return pltpu.make_async_copy(
            corr.at[0, 2 * p + a, pl.ds(2 * c, 2)], buf.at[k, slot_of(p, q)], own_sem.at[k]
        )

    def line_copy(k, d, arriving=False):
        c, a = divmod(k, 2)
        line = source(d) if arriving else p
        return pltpu.make_async_remote_copy(
            src_ref=corr.at[0, 2 * peer(d) + a, pl.ds(2 * c, 2)],
            dst_ref=buf.at[k, slot_of(line, q)],
            send_sem=line_s.at[k, d], recv_sem=line_r.at[k, d],
            device_id={"layer": 2 * peer(d) + q}, device_id_type=MESH,
        )

    def part_copy(k, d, arriving=False):
        slot = slot_of(source(d), 1 - q if arriving else q)
        return pltpu.make_async_remote_copy(
            src_ref=buf.at[k, slot], dst_ref=buf.at[k, slot],
            send_sem=part_s.at[k, d], recv_sem=part_r.at[k, d],
            device_id=partner, device_id_type=MESH,
        )

    def halo_copy(k, side):
        first = SHIFT_MAX if side == 0 else energies
        landing = SHIFT_MAX + energies if side == 0 else 0
        return pltpu.make_async_remote_copy(
            src_ref=buf.at[k, pl.ds(first, SHIFT_MAX)],
            dst_ref=buf.at[k, pl.ds(landing, SHIFT_MAX)],
            send_sem=halo_s.at[k, side], recv_sem=halo_r.at[k, side],
            device_id={"energy": e - 1 if side == 0 else e + 1}, device_id_type=MESH,
        )

    def ret_own_copy():
        return pltpu.make_async_copy(ret.at[0, pl.ds(2 * p, 2)], green.at[p], ret_own)

    def ret_copy(d, arriving=False):
        line = source(d) if arriving else p
        return pltpu.make_async_remote_copy(
            src_ref=ret.at[0, pl.ds(2 * peer(d), 2)], dst_ref=green.at[line],
            send_sem=ret_s.at[d], recv_sem=ret_r.at[d],
            device_id={"layer": 2 * peer(d) + q}, device_id_type=MESH,
        )

    def side_copies(arriving=False):
        at = 1 - q if arriving else q
        return (
            pltpu.make_async_remote_copy(
                src_ref=coupling.at[0], dst_ref=volt.at[at],
                send_sem=side_sem.at[0], recv_sem=side_sem.at[1],
                device_id=partner, device_id_type=MESH,
            ),
            pltpu.make_async_remote_copy(
                src_ref=alive.at[at], dst_ref=alive.at[at],
                send_sem=side_sem.at[2], recv_sem=side_sem.at[3],
                device_id=partner, device_id_type=MESH,
            ),
        )

    def side_own():
        return pltpu.make_async_copy(coupling.at[0], volt.at[q], side_sem.at[4])

    def chain_copy(c, i):
        return pltpu.make_async_remote_copy(
            src_ref=xout.at[c, 1, i], dst_ref=xin.at[c, i],
            send_sem=chain_s.at[c, i], recv_sem=chain_r.at[c, i],
            device_id={"layer": lax.rem(index + 2, 2 * lines)}, device_id_type=MESH,
        )

    def out_own(c, i):
        return pltpu.make_async_copy(
            xout.at[c, q, i], out.at[2 * i + q, 0, pl.ds(2 * c, 2)], out_sem.at[c, i]
        )

    def out_copy(c, i, arriving=False):
        parity = 1 - q if arriving else q
        return pltpu.make_async_remote_copy(
            src_ref=xout.at[c, 1 - q, i], dst_ref=out.at[2 * i + parity, 0, pl.ds(2 * c, 2)],
            send_sem=out_s.at[c, i], recv_sem=out_r.at[c, i],
            device_id=partner, device_id_type=MESH,
        )

    def start_line(k):
        own_copy(k).start()
        for d in range(1, lines):
            line_copy(k, d).start()

    def arrival(t):
        line = jnp.where(p < lines // 2, t, lines - 1 - t)
        return line, lax.rem(p + lines - line, lines)

    def pass_on(k):
        own_copy(k).wait()
        part_copy(k, 0).start()
        for t in range(lines):
            line, d = arrival(t)

            @pl.when(line != p)
            def _():
                line_copy(k, d, True).wait_recv()
                part_copy(k, d).start()

    def start_halo(k):
        for d in range(lines):
            part_copy(k, d, True).wait_recv()

        @pl.when(e > 0)
        def _():
            halo_copy(k, 0).start()

        @pl.when(e < groups - 1)
        def _():
            halo_copy(k, 1).start()

    def self_energy(k):
        c, a = divmod(k, 2)

        @pl.when(e < groups - 1)
        def _():
            halo_copy(k, 0).wait_recv()

        @pl.when(e > 0)
        def _():
            halo_copy(k, 1).wait_recv()

        absorb, emit = tap_weights(shifts, strengths)
        below, above = (absorb, emit) if c == 0 else (emit, absorb)
        count = alive[a, 0:1, :]
        column = lax.broadcasted_iota(jnp.int32, (ROWS, orbitals), 1)
        row = lax.broadcasted_iota(jnp.int32, (ROWS, orbitals), 0)
        tiles = orbitals // ROWS

        def one(step, carry):
            i = step // (2 * tiles)
            component = lax.rem(step // tiles, 2)
            base = pl.multiple_of(lax.rem(step, tiles) * ROWS, ROWS)
            here = slot_of(i, q)
            total = jnp.zeros((ROWS, orbitals), jnp.float32)
            for d in range(SHIFT_MAX):
                low = buf[k, here - d - 1, component, pl.ds(base, ROWS), :].astype(jnp.float32)
                high = buf[k, here + d + 1, component, pl.ds(base, ROWS), :].astype(jnp.float32)
                total = total + (below[d] * low + above[d] * high)
            keep = (row + base < count) & (column < count)
            sigma[k, i, component, pl.ds(base, ROWS), :] = jnp.where(keep, total, 0.0).astype(half)
            return carry

        lax.fori_loop(0, lines * 2 * tiles, one, 0)

    def advance(c, a, i, previous):
        k = 2 * c + a
        v = volt[a]
        g_real = green[i, a, 0]
        g_imag = green[i, a, 1]
        halfway = [dot_t(previous[n], v).astype(half) for n in range(2)]
        src = [
            (sigma[k, i, n].astype(jnp.float32) + dot(v, halfway[n])).astype(half) for n in range(2)
        ]
        inner_real = (dot(g_real, src[0]) - dot(g_imag, src[1])).astype(half)
        inner_imag = (dot(g_real, src[1]) + dot(g_imag, src[0])).astype(half)
        xout[c, a, i, 0] = (dot_t(inner_real, g_real) + dot_t(inner_imag, g_imag)).astype(half)
        xout[c, a, i, 1] = (dot_t(inner_imag, g_real) - dot_t(inner_real, g_imag)).astype(half)

    def sweep_energy(i, carry):
        @pl.when(i == p)
        def _():
            ret_own_copy().wait()

        @pl.when(i != p)
        def _():
            ret_copy(lax.rem(p + lines - i, lines), True).wait_recv()

        for c in range(2):
            @pl.when(p == 0)
            def _(c=c):
                xin[c, i] = buf[2 * c, slot_of(i, q)]

            @pl.when(p > 0)
            def _(c=c):
                chain_copy(c, i).wait_recv()

            advance(c, 0, i, xin.at[c, i])
            advance(c, 1, i, xout.at[c, 0, i])

            @pl.when(p < lines - 1)
            def _(c=c):
                if c == 1:
                    chain_copy(0, i).wait_send()
                else:
                    @pl.when(i > 0)
                    def _():
                        chain_copy(1, i - 1).wait_send()

                chain_copy(c, i).start()

            out_copy(c, i).start()
            out_own(c, i).start()
        return carry

    start_line(0)
    alive[q] = jnp.full(alive.shape[1:], orbital_count[0], jnp.int32)
    start_line(1)
    side_own().start()
    for copy in side_copies():
        copy.start()

    for at, edge in ((0, 0), (SHIFT_MAX + energies, groups - 1)):
        @pl.when(e == edge)
        def _(at=at):
            def clear(step, carry):
                k = step // SHIFT_MAX
                slot = at + lax.rem(step, SHIFT_MAX)
                buf[k, slot] = jnp.zeros(buf.shape[2:], half)
                return carry

            lax.fori_loop(0, 4 * SHIFT_MAX, clear, 0)

    def start_ret():
        ret_own_copy().start()
        for d in range(1, lines):
            ret_copy(d).start()

    pass_on(0)
    start_line(2)
    pass_on(1)
    start_line(3)
    start_halo(0)
    pass_on(2)
    start_ret()
    start_halo(1)
    side_own().wait()
    for copy in side_copies(True):
        copy.wait_recv()
    self_energy(0)
    pass_on(3)
    start_halo(2)
    self_energy(1)
    start_halo(3)
    self_energy(2)
    self_energy(3)
    lax.fori_loop(0, lines, sweep_energy, 0)

    for copy in side_copies():
        copy.wait_send()
    for d in range(1, lines):
        ret_copy(d).wait_send()
        for k in range(4):
            line_copy(k, d).wait_send()
    for k in range(4):
        for d in range(lines):
            part_copy(k, d).wait_send()

        @pl.when(e > 0)
        def _(k=k):
            halo_copy(k, 0).wait_send()

        @pl.when(e < groups - 1)
        def _(k=k):
            halo_copy(k, 1).wait_send()

    @pl.when(p < lines - 1)
    def _():
        chain_copy(1, lines - 1).wait_send()

    for c in range(2):
        def finish(i, carry, c=c):
            out_own(c, i).wait()
            out_copy(c, i).wait_send()
            out_copy(c, i, True).wait_recv()
            return carry

        lax.fori_loop(0, lines, finish, 0)


def body(correlations, retarded, coupling, phonon_shifts, phonon_coupling, layer_orbitals):
    groups = lax.axis_size("energy")
    energies = lax.axis_size("layer")
    lines = energies // 2
    orbitals = correlations.shape[-1]
    block = (2, orbitals, orbitals)
    low = jnp.bfloat16
    shapes = [
        (4, energies + 2 * SHIFT_MAX) + block,
        (lines, 2) + block,
        (2, orbitals, orbitals),
        None,
        (4, lines) + block,
        (2, lines) + block,
        (2, 2, lines) + block,
    ]
    scratch = [
        pltpu.VMEM((2, 8, orbitals), jnp.int32) if shape is None else pltpu.VMEM(shape, low)
        for shape in shapes
    ]
    blocks = 4 * (energies + 2 * SHIFT_MAX) + 12 * lines + 1
    dma = pltpu.SemaphoreType.DMA
    semaphores = [
        dma((4,)), dma((4, lines)), dma((4, lines)), dma((4, lines)), dma((4, lines)),
        dma((4, 2)), dma((4, 2)),
        dma(()), dma((lines,)), dma((lines,)), dma((6,)),
        dma((2, lines)), dma((2, lines)), dma((2, lines)), dma((2, lines)), dma((2, lines)),
    ]
    large = pl.BlockSpec(memory_space=pltpu.HBM)
    anywhere = pl.BlockSpec(memory_space=pl.ANY)
    return pl.pallas_call(
        functools.partial(kernel, groups, lines, orbitals),
        out_shape=jax.ShapeDtypeStruct((energies, 1, 4, orbitals, orbitals), low),
        in_specs=[pl.BlockSpec(memory_space=pltpu.SMEM)] * 3 + [large] * 3,
        out_specs=anywhere,
        scratch_shapes=scratch + semaphores,
        compiler_params=pltpu.CompilerParams(
            collective_id=0, has_side_effects=True,
            vmem_limit_bytes=blocks * 4 * orbitals * orbitals + (6 << 20),
        ),
        cost_estimate=pl.CostEstimate(
            flops=lines * 4 * 12 * 2 * orbitals**3, bytes_accessed=12 << 20, transcendentals=0
        ),
    )(phonon_shifts, phonon_coupling, layer_orbitals, correlations, retarded, coupling)


def solution(mesh):
    return jax.shard_map(
        body,
        mesh=mesh,
        in_specs=(
            P(("energy", "layer"), None, None, None, None),
            P(("energy", "layer"), None, None, None, None),
            P("layer", None, None),
            P(),
            P(),
            P("layer"),
        ),
        out_specs=P("energy", "layer", None, None, None),
        check_vma=False,
    )
```

```python
import functools
import math

import jax
import jax.numpy as jnp
from jax import lax
from jax.experimental import pallas as pl
from jax.experimental.pallas import tpu as pltpu
from jax.sharding import PartitionSpec as P

SHIFT_MAX = 4
MESH = pl.DeviceIdType.MESH
ROWS = 32

bose_ratio = 0.5


def tap_weights(shifts, strengths):
    absorb, emit = [], []
    for distance in range(1, SHIFT_MAX + 1):
        strength = jnp.float32(0)
        for mode in range(shifts.shape[0]):
            strength += jnp.where(shifts[mode] == distance, strengths[mode], jnp.float32(0))
        occupation = 1.0 / math.expm1(bose_ratio * distance)
        absorb.append(strength * jnp.float32(occupation))
        emit.append(strength * jnp.float32(occupation + 1.0))
    return absorb, emit


def dot(a, b):
    return lax.dot_general(a, b, (((1,), (0,)), ((), ())), preferred_element_type=jnp.float32)


def dot_t(a, b):
    return lax.dot_general(a, b, (((1,), (1,)), ((), ())), preferred_element_type=jnp.float32)


def kernel(
    groups, lines, orbitals,
    shifts, strengths, orbital_count, corr, ret, coupling, out,
    buf, green, volt, alive, sigma, xin, xout,
    own_sem, line_s, line_r, part_s, part_r, halo_s, halo_r,
    ret_own, ret_s, ret_r, side_sem, chain_s, chain_r, out_sem, out_s, out_r,
):
    energies = 2 * lines
    e = lax.axis_index("energy")
    index = lax.axis_index("layer")
    p = index // 2
    q = lax.rem(index, 2)
    partner = {"layer": 2 * p + (1 - q)}
    half = jnp.bfloat16

    def peer(d):
        return lax.rem(p + d, lines)

    def source(d):
        return lax.rem(p + lines - d, lines)

    barrier = pltpu.get_barrier_semaphore()
    for d in range(1, lines):
        pl.semaphore_signal(barrier, inc=1, device_id={"layer": 2 * peer(d) + q}, device_id_type=MESH)
    pl.semaphore_signal(barrier, inc=1, device_id=partner, device_id_type=MESH)

    @pl.when(e > 0)
    def _():
        pl.semaphore_signal(barrier, inc=1, device_id={"energy": e - 1}, device_id_type=MESH)

    @pl.when(e < groups - 1)
    def _():
        pl.semaphore_signal(barrier, inc=1, device_id={"energy": e + 1}, device_id_type=MESH)

    beside = (e > 0).astype(jnp.int32) + (e < groups - 1).astype(jnp.int32)
    pl.semaphore_wait(barrier, lines + beside)

    def slot_of(line, parity):
        return SHIFT_MAX + 2 * line + parity

    def own_copy(k):
        c, a = divmod(k, 2)
        return pltpu.make_async_copy(
            corr.at[0, 2 * p + a, pl.ds(2 * c, 2)], buf.at[k, slot_of(p, q)], own_sem.at[k]
        )

    def line_copy(k, d, arriving=False):
        c, a = divmod(k, 2)
        line = source(d) if arriving else p
        return pltpu.make_async_remote_copy(
            src_ref=corr.at[0, 2 * peer(d) + a, pl.ds(2 * c, 2)],
            dst_ref=buf.at[k, slot_of(line, q)],
            send_sem=line_s.at[k, d], recv_sem=line_r.at[k, d],
            device_id={"layer": 2 * peer(d) + q}, device_id_type=MESH,
        )

    def part_copy(k, d, arriving=False):
        slot = slot_of(source(d), 1 - q if arriving else q)
        return pltpu.make_async_remote_copy(
            src_ref=buf.at[k, slot], dst_ref=buf.at[k, slot],
            send_sem=part_s.at[k, d], recv_sem=part_r.at[k, d],
            device_id=partner, device_id_type=MESH,
        )

    def halo_copy(k, side):
        first = SHIFT_MAX if side == 0 else energies
        landing = SHIFT_MAX + energies if side == 0 else 0
        return pltpu.make_async_remote_copy(
            src_ref=buf.at[k, pl.ds(first, SHIFT_MAX)],
            dst_ref=buf.at[k, pl.ds(landing, SHIFT_MAX)],
            send_sem=halo_s.at[k, side], recv_sem=halo_r.at[k, side],
            device_id={"energy": e - 1 if side == 0 else e + 1}, device_id_type=MESH,
        )

    def ret_own_copy():
        return pltpu.make_async_copy(ret.at[0, pl.ds(2 * p, 2)], green.at[p], ret_own)

    def ret_copy(d, arriving=False):
        line = source(d) if arriving else p
        return pltpu.make_async_remote_copy(
            src_ref=ret.at[0, pl.ds(2 * peer(d), 2)], dst_ref=green.at[line],
            send_sem=ret_s.at[d], recv_sem=ret_r.at[d],
            device_id={"layer": 2 * peer(d) + q}, device_id_type=MESH,
        )

    def side_copies(arriving=False):
        at = 1 - q if arriving else q
        return (
            pltpu.make_async_remote_copy(
                src_ref=coupling.at[0], dst_ref=volt.at[at],
                send_sem=side_sem.at[0], recv_sem=side_sem.at[1],
                device_id=partner, device_id_type=MESH,
            ),
            pltpu.make_async_remote_copy(
                src_ref=alive.at[at], dst_ref=alive.at[at],
                send_sem=side_sem.at[2], recv_sem=side_sem.at[3],
                device_id=partner, device_id_type=MESH,
            ),
        )

    def side_own():
        return pltpu.make_async_copy(coupling.at[0], volt.at[q], side_sem.at[4])

    def chain_copy(c, i):
        return pltpu.make_async_remote_copy(
            src_ref=xout.at[c, 1, i], dst_ref=xin.at[c, i],
            send_sem=chain_s.at[c, i], recv_sem=chain_r.at[c, i],
            device_id={"layer": lax.rem(index + 2, 2 * lines)}, device_id_type=MESH,
        )

    def out_own(c, i):
        return pltpu.make_async_copy(
            xout.at[c, q, i], out.at[2 * i + q, 0, pl.ds(2 * c, 2)], out_sem.at[c, i]
        )

    def out_copy(c, i, arriving=False):
        parity = 1 - q if arriving else q
        return pltpu.make_async_remote_copy(
            src_ref=xout.at[c, 1 - q, i], dst_ref=out.at[2 * i + parity, 0, pl.ds(2 * c, 2)],
            send_sem=out_s.at[c, i], recv_sem=out_r.at[c, i],
            device_id=partner, device_id_type=MESH,
        )

    def start_line(k):
        own_copy(k).start()
        for d in range(1, lines):
            line_copy(k, d).start()

    def arrival(t):
        line = jnp.where(p < lines // 2, t, lines - 1 - t)
        return line, lax.rem(p + lines - line, lines)

    def pass_on(k):
        own_copy(k).wait()
        part_copy(k, 0).start()
        for t in range(lines):
            line, d = arrival(t)

            @pl.when(line != p)
            def _():
                line_copy(k, d, True).wait_recv()
                part_copy(k, d).start()

    def start_halo(k):
        for d in range(lines):
            part_copy(k, d, True).wait_recv()

        @pl.when(e > 0)
        def _():
            halo_copy(k, 0).start()

        @pl.when(e < groups - 1)
        def _():
            halo_copy(k, 1).start()

    def self_energy(k):
        c, a = divmod(k, 2)

        @pl.when(e < groups - 1)
        def _():
            halo_copy(k, 0).wait_recv()

        @pl.when(e > 0)
        def _():
            halo_copy(k, 1).wait_recv()

        absorb, emit = tap_weights(shifts, strengths)
        below, above = (absorb, emit) if c == 0 else (emit, absorb)
        count = alive[a, 0:1, :]
        column = lax.broadcasted_iota(jnp.int32, (ROWS, orbitals), 1)
        row = lax.broadcasted_iota(jnp.int32, (ROWS, orbitals), 0)
        tiles = orbitals // ROWS

        def one(step, carry):
            i = step // (2 * tiles)
            component = lax.rem(step // tiles, 2)
            base = pl.multiple_of(lax.rem(step, tiles) * ROWS, ROWS)
            here = slot_of(i, q)
            total = jnp.zeros((ROWS, orbitals), jnp.float32)
            for d in range(SHIFT_MAX):
                low = buf[k, here - d - 1, component, pl.ds(base, ROWS), :].astype(jnp.float32)
                high = buf[k, here + d + 1, component, pl.ds(base, ROWS), :].astype(jnp.float32)
                total = total + (below[d] * low + above[d] * high)
            keep = (row + base < count) & (column < count)
            sigma[k, i, component, pl.ds(base, ROWS), :] = jnp.where(keep, total, 0.0).astype(half)
            return carry

        lax.fori_loop(0, lines * 2 * tiles, one, 0)

    def advance(c, a, i, previous):
        k = 2 * c + a
        v = volt[a]
        g_real = green[i, a, 0]
        g_imag = green[i, a, 1]
        halfway = [dot_t(previous[n], v).astype(half) for n in range(2)]
        src = [
            (sigma[k, i, n].astype(jnp.float32) + dot(v, halfway[n])).astype(half) for n in range(2)
        ]
        inner_real = (dot(g_real, src[0]) - dot(g_imag, src[1])).astype(half)
        inner_imag = (dot(g_real, src[1]) + dot(g_imag, src[0])).astype(half)
        xout[c, a, i, 0] = (dot_t(inner_real, g_real) + dot_t(inner_imag, g_imag)).astype(half)
        xout[c, a, i, 1] = (dot_t(inner_imag, g_real) - dot_t(inner_real, g_imag)).astype(half)

    def sweep_energy(i, carry):
        @pl.when(i == p)
        def _():
            ret_own_copy().wait()

        @pl.when(i != p)
        def _():
            ret_copy(lax.rem(p + lines - i, lines), True).wait_recv()

        for c in range(2):
            @pl.when(p == 0)
            def _(c=c):
                xin[c, i] = buf[2 * c, slot_of(i, q)]

            @pl.when(p > 0)
            def _(c=c):
                chain_copy(c, i).wait_recv()

            advance(c, 0, i, xin.at[c, i])

            @pl.when(q == 1)
            def _(c=c):
                out_copy(c, i).start()

            advance(c, 1, i, xout.at[c, 0, i])

            @pl.when(q == 0)
            def _(c=c):
                out_copy(c, i).start()

            @pl.when(p < lines - 1)
            def _(c=c):
                if c == 1:
                    chain_copy(0, i).wait_send()
                else:
                    @pl.when(i > 0)
                    def _():
                        chain_copy(1, i - 1).wait_send()

                chain_copy(c, i).start()

            out_own(c, i).start()
        return carry

    start_line(0)
    alive[q] = jnp.full(alive.shape[1:], orbital_count[0], jnp.int32)
    start_line(1)
    start_line(2)
    side_own().start()
    for copy in side_copies():
        copy.start()

    for at, edge in ((0, 0), (SHIFT_MAX + energies, groups - 1)):
        @pl.when(e == edge)
        def _(at=at):
            def clear(step, carry):
                k = step // SHIFT_MAX
                slot = at + lax.rem(step, SHIFT_MAX)
                buf[k, slot] = jnp.zeros(buf.shape[2:], half)
                return carry

            lax.fori_loop(0, 4 * SHIFT_MAX, clear, 0)

    def start_ret():
        ret_own_copy().start()
        for d in range(1, lines):
            ret_copy(d).start()

    pass_on(0)
    start_line(3)
    pass_on(1)
    start_ret()
    start_halo(0)
    pass_on(2)
    start_halo(1)
    side_own().wait()
    for copy in side_copies(True):
        copy.wait_recv()
    self_energy(0)
    pass_on(3)
    start_halo(2)
    self_energy(1)
    start_halo(3)
    self_energy(2)
    self_energy(3)
    lax.fori_loop(0, lines, sweep_energy, 0)

    for copy in side_copies():
        copy.wait_send()
    for d in range(1, lines):
        ret_copy(d).wait_send()
        for k in range(4):
            line_copy(k, d).wait_send()
    for k in range(4):
        for d in range(lines):
            part_copy(k, d).wait_send()

        @pl.when(e > 0)
        def _(k=k):
            halo_copy(k, 0).wait_send()

        @pl.when(e < groups - 1)
        def _(k=k):
            halo_copy(k, 1).wait_send()

    @pl.when(p < lines - 1)
    def _():
        chain_copy(1, lines - 1).wait_send()

    for c in range(2):
        def finish(i, carry, c=c):
            out_own(c, i).wait()
            out_copy(c, i).wait_send()
            out_copy(c, i, True).wait_recv()
            return carry

        lax.fori_loop(0, lines, finish, 0)


def body(correlations, retarded, coupling, phonon_shifts, phonon_coupling, layer_orbitals):
    groups = lax.axis_size("energy")
    energies = lax.axis_size("layer")
    lines = energies // 2
    orbitals = correlations.shape[-1]
    block = (2, orbitals, orbitals)
    low = jnp.bfloat16
    shapes = [
        (4, energies + 2 * SHIFT_MAX) + block,
        (lines, 2) + block,
        (2, orbitals, orbitals),
        None,
        (4, lines) + block,
        (2, lines) + block,
        (2, 2, lines) + block,
    ]
    scratch = [
        pltpu.VMEM((2, 8, orbitals), jnp.int32) if shape is None else pltpu.VMEM(shape, low)
        for shape in shapes
    ]
    dma = pltpu.SemaphoreType.DMA
    semaphores = [
        dma((4,)), dma((4, lines)), dma((4, lines)), dma((4, lines)), dma((4, lines)),
        dma((4, 2)), dma((4, 2)),
        dma(()), dma((lines,)), dma((lines,)), dma((6,)),
        dma((2, lines)), dma((2, lines)), dma((2, lines)), dma((2, lines)), dma((2, lines)),
    ]
    large = pl.BlockSpec(memory_space=pltpu.HBM)
    anywhere = pl.BlockSpec(memory_space=pl.ANY)
    return pl.pallas_call(
        functools.partial(kernel, groups, lines, orbitals),
        out_shape=jax.ShapeDtypeStruct((energies, 1, 4, orbitals, orbitals), low),
        in_specs=[pl.BlockSpec(memory_space=pltpu.SMEM)] * 3 + [large] * 3,
        out_specs=anywhere,
        scratch_shapes=scratch + semaphores,
        compiler_params=pltpu.CompilerParams(
            collective_id=0, has_side_effects=True,
            vmem_limit_bytes=60 << 20,
        ),
        cost_estimate=pl.CostEstimate(
            flops=lines * 4 * 12 * 2 * orbitals**3, bytes_accessed=12 << 20, transcendentals=0
        ),
    )(phonon_shifts, phonon_coupling, layer_orbitals, correlations, retarded, coupling)


def solution(mesh):
    return jax.shard_map(
        body,
        mesh=mesh,
        in_specs=(
            P(("energy", "layer"), None, None, None, None),
            P(("energy", "layer"), None, None, None, None),
            P("layer", None, None),
            P(),
            P(),
            P("layer"),
        ),
        out_specs=P("energy", "layer", None, None, None),
        check_vma=False,
    )
```

```python
import functools
import math

import jax
import jax.numpy as jnp
from jax import lax
from jax.experimental import pallas as pl
from jax.experimental.pallas import tpu as pltpu
from jax.sharding import PartitionSpec as P

SHIFT_MAX = 4
MESH = pl.DeviceIdType.MESH
ROWS = 32

bose_ratio = 0.5


def tap_weights(shifts, strengths):
    absorb, emit = [], []
    for distance in range(1, SHIFT_MAX + 1):
        strength = jnp.float32(0)
        for mode in range(shifts.shape[0]):
            strength += jnp.where(shifts[mode] == distance, strengths[mode], jnp.float32(0))
        occupation = 1.0 / math.expm1(bose_ratio * distance)
        absorb.append(strength * jnp.float32(occupation))
        emit.append(strength * jnp.float32(occupation + 1.0))
    return absorb, emit


def dot(a, b):
    return lax.dot_general(a, b, (((1,), (0,)), ((), ())), preferred_element_type=jnp.float32)


def dot_t(a, b):
    return lax.dot_general(a, b, (((1,), (1,)), ((), ())), preferred_element_type=jnp.float32)


def kernel(
    groups, lines, orbitals,
    shifts, strengths, orbital_count, corr, ret, coupling, out,
    buf, green, volt, alive, sigma, xin, xout,
    own_sem, line_s, line_r, part_s, part_r, halo_s, halo_r,
    ret_own, ret_s, ret_r, side_sem, chain_s, chain_r, out_sem, out_s, out_r,
):
    energies = 2 * lines
    e = lax.axis_index("energy")
    index = lax.axis_index("layer")
    p = index // 2
    q = lax.rem(index, 2)
    partner = {"layer": 2 * p + (1 - q)}
    half = jnp.bfloat16

    def peer(d):
        return lax.rem(p + d, lines)

    def source(d):
        return lax.rem(p + lines - d, lines)

    barrier = pltpu.get_barrier_semaphore()
    for d in range(1, lines):
        pl.semaphore_signal(barrier, inc=1, device_id={"layer": 2 * peer(d) + q}, device_id_type=MESH)
    pl.semaphore_signal(barrier, inc=1, device_id=partner, device_id_type=MESH)

    @pl.when(e > 0)
    def _():
        pl.semaphore_signal(barrier, inc=1, device_id={"energy": e - 1}, device_id_type=MESH)

    @pl.when(e < groups - 1)
    def _():
        pl.semaphore_signal(barrier, inc=1, device_id={"energy": e + 1}, device_id_type=MESH)

    beside = (e > 0).astype(jnp.int32) + (e < groups - 1).astype(jnp.int32)
    pl.semaphore_wait(barrier, lines + beside)

    def slot_of(line, parity):
        return SHIFT_MAX + 2 * line + parity

    def own_copy(k):
        c, a = divmod(k, 2)
        return pltpu.make_async_copy(
            corr.at[0, 2 * p + a, pl.ds(2 * c, 2)], buf.at[k, slot_of(p, q)], own_sem.at[k]
        )

    def line_copy(k, d, arriving=False):
        c, a = divmod(k, 2)
        line = source(d) if arriving else p
        return pltpu.make_async_remote_copy(
            src_ref=corr.at[0, 2 * peer(d) + a, pl.ds(2 * c, 2)],
            dst_ref=buf.at[k, slot_of(line, q)],
            send_sem=line_s.at[k, d], recv_sem=line_r.at[k, d],
            device_id={"layer": 2 * peer(d) + q}, device_id_type=MESH,
        )

    def part_copy(k, d, arriving=False):
        slot = slot_of(source(d), 1 - q if arriving else q)
        return pltpu.make_async_remote_copy(
            src_ref=buf.at[k, slot], dst_ref=buf.at[k, slot],
            send_sem=part_s.at[k, d], recv_sem=part_r.at[k, d],
            device_id=partner, device_id_type=MESH,
        )

    def halo_copy(k, side):
        first = SHIFT_MAX if side == 0 else energies
        landing = SHIFT_MAX + energies if side == 0 else 0
        return pltpu.make_async_remote_copy(
            src_ref=buf.at[k, pl.ds(first, SHIFT_MAX)],
            dst_ref=buf.at[k, pl.ds(landing, SHIFT_MAX)],
            send_sem=halo_s.at[k, side], recv_sem=halo_r.at[k, side],
            device_id={"energy": e - 1 if side == 0 else e + 1}, device_id_type=MESH,
        )

    def ret_own_copy():
        return pltpu.make_async_copy(ret.at[0, pl.ds(2 * p, 2)], green.at[p], ret_own)

    def ret_copy(d, arriving=False):
        line = source(d) if arriving else p
        return pltpu.make_async_remote_copy(
            src_ref=ret.at[0, pl.ds(2 * peer(d), 2)], dst_ref=green.at[line],
            send_sem=ret_s.at[d], recv_sem=ret_r.at[d],
            device_id={"layer": 2 * peer(d) + q}, device_id_type=MESH,
        )

    def side_copies(arriving=False):
        at = 1 - q if arriving else q
        return (
            pltpu.make_async_remote_copy(
                src_ref=coupling.at[0], dst_ref=volt.at[at],
                send_sem=side_sem.at[0], recv_sem=side_sem.at[1],
                device_id=partner, device_id_type=MESH,
            ),
            pltpu.make_async_remote_copy(
                src_ref=alive.at[at], dst_ref=alive.at[at],
                send_sem=side_sem.at[2], recv_sem=side_sem.at[3],
                device_id=partner, device_id_type=MESH,
            ),
        )

    def side_own():
        return pltpu.make_async_copy(coupling.at[0], volt.at[q], side_sem.at[4])

    def chain_copy(c, i):
        return pltpu.make_async_remote_copy(
            src_ref=xout.at[c, 1, i], dst_ref=xin.at[c, i],
            send_sem=chain_s.at[c, i], recv_sem=chain_r.at[c, i],
            device_id={"layer": lax.rem(index + 2, 2 * lines)}, device_id_type=MESH,
        )

    def out_own(c, i):
        return pltpu.make_async_copy(
            xout.at[c, q, i], out.at[2 * i + q, 0, pl.ds(2 * c, 2)], out_sem.at[c, i]
        )

    def out_copy(c, i, arriving=False):
        parity = 1 - q if arriving else q
        return pltpu.make_async_remote_copy(
            src_ref=xout.at[c, 1 - q, i], dst_ref=out.at[2 * i + parity, 0, pl.ds(2 * c, 2)],
            send_sem=out_s.at[c, i], recv_sem=out_r.at[c, i],
            device_id=partner, device_id_type=MESH,
        )

    def start_line(k):
        own_copy(k).start()
        for d in range(1, lines):
            line_copy(k, d).start()

    def arrival(t):
        line = jnp.where(p < lines // 2, t, lines - 1 - t)
        return line, lax.rem(p + lines - line, lines)

    def pass_on(k):
        own_copy(k).wait()
        part_copy(k, 0).start()
        for t in range(lines):
            line, d = arrival(t)

            @pl.when(line != p)
            def _():
                line_copy(k, d, True).wait_recv()
                part_copy(k, d).start()

    def start_halo(k):
        for d in range(lines):
            part_copy(k, d, True).wait_recv()

        @pl.when(e > 0)
        def _():
            halo_copy(k, 0).start()

        @pl.when(e < groups - 1)
        def _():
            halo_copy(k, 1).start()

    def self_energy(k):
        c, a = divmod(k, 2)

        @pl.when(e < groups - 1)
        def _():
            halo_copy(k, 0).wait_recv()

        @pl.when(e > 0)
        def _():
            halo_copy(k, 1).wait_recv()

        absorb, emit = tap_weights(shifts, strengths)
        below, above = (absorb, emit) if c == 0 else (emit, absorb)
        count = alive[a, 0:1, :]
        column = lax.broadcasted_iota(jnp.int32, (ROWS, orbitals), 1)
        row = lax.broadcasted_iota(jnp.int32, (ROWS, orbitals), 0)
        tiles = orbitals // ROWS

        def one(step, carry):
            i = step // (2 * tiles)
            component = lax.rem(step // tiles, 2)
            base = pl.multiple_of(lax.rem(step, tiles) * ROWS, ROWS)
            here = slot_of(i, q)
            total = jnp.zeros((ROWS, orbitals), jnp.float32)
            for d in range(SHIFT_MAX):
                low = buf[k, here - d - 1, component, pl.ds(base, ROWS), :].astype(jnp.float32)
                high = buf[k, here + d + 1, component, pl.ds(base, ROWS), :].astype(jnp.float32)
                total = total + (below[d] * low + above[d] * high)
            keep = (row + base < count) & (column < count)
            sigma[k, i, component, pl.ds(base, ROWS), :] = jnp.where(keep, total, 0.0).astype(half)
            return carry

        lax.fori_loop(0, lines * 2 * tiles, one, 0)

    def advance(c, a, i, previous):
        k = 2 * c + a
        v = volt[a]
        g_real = green[i, a, 0]
        g_imag = green[i, a, 1]
        halfway = [dot_t(previous[n], v).astype(half) for n in range(2)]
        src = [
            (sigma[k, i, n].astype(jnp.float32) + dot(v, halfway[n])).astype(half) for n in range(2)
        ]
        inner_real = (dot(g_real, src[0]) - dot(g_imag, src[1])).astype(half)
        inner_imag = (dot(g_real, src[1]) + dot(g_imag, src[0])).astype(half)
        xout[c, a, i, 0] = (dot_t(inner_real, g_real) + dot_t(inner_imag, g_imag)).astype(half)
        xout[c, a, i, 1] = (dot_t(inner_imag, g_real) - dot_t(inner_real, g_imag)).astype(half)

    def sweep_energy(i, carry):
        @pl.when(i == p)
        def _():
            ret_own_copy().wait()

        @pl.when(i != p)
        def _():
            ret_copy(lax.rem(p + lines - i, lines), True).wait_recv()

        for c in range(2):
            @pl.when(p == 0)
            def _(c=c):
                xin[c, i] = buf[2 * c, slot_of(i, q)]

            @pl.when(p > 0)
            def _(c=c):
                chain_copy(c, i).wait_recv()

            advance(c, 0, i, xin.at[c, i])

            @pl.when(q == 1)
            def _(c=c):
                out_copy(c, i).start()

            advance(c, 1, i, xout.at[c, 0, i])

            @pl.when(q == 0)
            def _(c=c):
                out_copy(c, i).start()

            @pl.when(p < lines - 1)
            def _(c=c):
                if c == 1:
                    chain_copy(0, i).wait_send()
                else:
                    @pl.when(i > 0)
                    def _():
                        chain_copy(1, i - 1).wait_send()

                chain_copy(c, i).start()

            out_own(c, i).start()
        return carry

    start_line(0)
    alive[q] = jnp.full(alive.shape[1:], orbital_count[0], jnp.int32)
    start_line(1)
    start_line(2)
    side_own().start()
    for copy in side_copies():
        copy.start()

    for at, edge in ((0, 0), (SHIFT_MAX + energies, groups - 1)):
        @pl.when(e == edge)
        def _(at=at):
            def clear(step, carry):
                k = step // SHIFT_MAX
                slot = at + lax.rem(step, SHIFT_MAX)
                buf[k, slot] = jnp.zeros(buf.shape[2:], half)
                return carry

            lax.fori_loop(0, 4 * SHIFT_MAX, clear, 0)

    def start_ret():
        ret_own_copy().start()
        for d in range(1, lines):
            ret_copy(d).start()

    pass_on(0)
    start_line(3)
    pass_on(1)
    start_ret()
    start_halo(0)
    pass_on(2)
    start_halo(1)
    side_own().wait()
    for copy in side_copies(True):
        copy.wait_recv()
    self_energy(0)
    pass_on(3)
    start_halo(2)
    self_energy(1)
    start_halo(3)
    self_energy(2)
    self_energy(3)
    lax.fori_loop(0, lines, sweep_energy, 0)

    for copy in side_copies():
        copy.wait_send()
    for d in range(1, lines):
        ret_copy(d).wait_send()
        for k in range(4):
            line_copy(k, d).wait_send()
    for k in range(4):
        for d in range(lines):
            part_copy(k, d).wait_send()

        @pl.when(e > 0)
        def _(k=k):
            halo_copy(k, 0).wait_send()

        @pl.when(e < groups - 1)
        def _(k=k):
            halo_copy(k, 1).wait_send()

    @pl.when(p < lines - 1)
    def _():
        chain_copy(1, lines - 1).wait_send()

    for c in range(2):
        def finish(i, carry, c=c):
            out_own(c, i).wait()
            out_copy(c, i).wait_send()
            out_copy(c, i, True).wait_recv()
            return carry

        lax.fori_loop(0, lines, finish, 0)


def body(correlations, retarded, coupling, phonon_shifts, phonon_coupling, layer_orbitals):
    groups = lax.axis_size("energy")
    energies = lax.axis_size("layer")
    lines = energies // 2
    orbitals = correlations.shape[-1]
    block = (2, orbitals, orbitals)
    low = jnp.bfloat16
    shapes = [
        (4, energies + 2 * SHIFT_MAX) + block,
        (lines, 2) + block,
        (2, orbitals, orbitals),
        None,
        (4, lines) + block,
        (2, lines) + block,
        (2, 2, lines) + block,
    ]
    scratch = [
        pltpu.VMEM((2, 8, orbitals), jnp.int32) if shape is None else pltpu.VMEM(shape, low)
        for shape in shapes
    ]
    blocks = 4 * (energies + 2 * SHIFT_MAX) + 12 * lines + 1
    dma = pltpu.SemaphoreType.DMA
    semaphores = [
        dma((4,)), dma((4, lines)), dma((4, lines)), dma((4, lines)), dma((4, lines)),
        dma((4, 2)), dma((4, 2)),
        dma(()), dma((lines,)), dma((lines,)), dma((6,)),
        dma((2, lines)), dma((2, lines)), dma((2, lines)), dma((2, lines)), dma((2, lines)),
    ]
    large = pl.BlockSpec(memory_space=pltpu.HBM)
    anywhere = pl.BlockSpec(memory_space=pl.ANY)
    return pl.pallas_call(
        functools.partial(kernel, groups, lines, orbitals),
        out_shape=jax.ShapeDtypeStruct((energies, 1, 4, orbitals, orbitals), low),
        in_specs=[pl.BlockSpec(memory_space=pltpu.SMEM)] * 3 + [large] * 3,
        out_specs=anywhere,
        scratch_shapes=scratch + semaphores,
        compiler_params=pltpu.CompilerParams(
            collective_id=0, has_side_effects=True,
            vmem_limit_bytes=blocks * 4 * orbitals * orbitals + (6 << 20),
        ),
        cost_estimate=pl.CostEstimate(
            flops=lines * 4 * 12 * 2 * orbitals**3, bytes_accessed=12 << 20, transcendentals=0
        ),
    )(phonon_shifts, phonon_coupling, layer_orbitals, correlations, retarded, coupling)


def solution(mesh):
    return jax.shard_map(
        body,
        mesh=mesh,
        in_specs=(
            P(("energy", "layer"), None, None, None, None),
            P(("energy", "layer"), None, None, None, None),
            P("layer", None, None),
            P(),
            P(),
            P("layer"),
        ),
        out_specs=P("energy", "layer", None, None, None),
        check_vma=False,
    )
```

```python
import functools
import math

import jax
import jax.numpy as jnp
from jax import lax
from jax.experimental import pallas as pl
from jax.experimental.pallas import tpu as pltpu
from jax.sharding import PartitionSpec as P

SHIFT_MAX = 4
MESH = pl.DeviceIdType.MESH
ROWS = 32

bose_ratio = 0.5


def tap_weights(shifts, strengths):
    absorb, emit = [], []
    for distance in range(1, SHIFT_MAX + 1):
        strength = jnp.float32(0)
        for mode in range(shifts.shape[0]):
            strength += jnp.where(shifts[mode] == distance, strengths[mode], jnp.float32(0))
        occupation = 1.0 / math.expm1(bose_ratio * distance)
        absorb.append(strength * jnp.float32(occupation))
        emit.append(strength * jnp.float32(occupation + 1.0))
    return absorb, emit


def dot(a, b):
    return lax.dot_general(a, b, (((1,), (0,)), ((), ())), preferred_element_type=jnp.float32)


def dot_t(a, b):
    return lax.dot_general(a, b, (((1,), (1,)), ((), ())), preferred_element_type=jnp.float32)


def kernel(
    groups, lines, orbitals,
    shifts, strengths, orbital_count, corr, ret, coupling, out,
    buf, green, volt, alive, sigma, xin, xout,
    own_sem, line_s, line_r, part_s, part_r, halo_s, halo_r,
    ret_own, ret_s, ret_r, side_sem, chain_s, chain_r, out_sem, out_s, out_r,
):
    energies = 2 * lines
    e = lax.axis_index("energy")
    index = lax.axis_index("layer")
    p = index // 2
    q = lax.rem(index, 2)
    partner = {"layer": 2 * p + (1 - q)}
    half = jnp.bfloat16

    def peer(d):
        return lax.rem(p + d, lines)

    def source(d):
        return lax.rem(p + lines - d, lines)

    barrier = pltpu.get_barrier_semaphore()
    for d in range(1, lines):
        pl.semaphore_signal(barrier, inc=1, device_id={"layer": 2 * peer(d) + q}, device_id_type=MESH)
    pl.semaphore_signal(barrier, inc=1, device_id=partner, device_id_type=MESH)

    @pl.when(e > 0)
    def _():
        pl.semaphore_signal(barrier, inc=1, device_id={"energy": e - 1}, device_id_type=MESH)

    @pl.when(e < groups - 1)
    def _():
        pl.semaphore_signal(barrier, inc=1, device_id={"energy": e + 1}, device_id_type=MESH)

    beside = (e > 0).astype(jnp.int32) + (e < groups - 1).astype(jnp.int32)
    pl.semaphore_wait(barrier, lines + beside)

    def slot_of(line, parity):
        return SHIFT_MAX + 2 * line + parity

    def own_copy(k):
        c, a = divmod(k, 2)
        return pltpu.make_async_copy(
            corr.at[0, 2 * p + a, pl.ds(2 * c, 2)], buf.at[k, slot_of(p, q)], own_sem.at[k]
        )

    def line_copy(k, d, arriving=False):
        c, a = divmod(k, 2)
        line = source(d) if arriving else p
        return pltpu.make_async_remote_copy(
            src_ref=corr.at[0, 2 * peer(d) + a, pl.ds(2 * c, 2)],
            dst_ref=buf.at[k, slot_of(line, q)],
            send_sem=line_s.at[k, d], recv_sem=line_r.at[k, d],
            device_id={"layer": 2 * peer(d) + q}, device_id_type=MESH,
        )

    def part_copy(k, d, arriving=False):
        slot = slot_of(source(d), 1 - q if arriving else q)
        return pltpu.make_async_remote_copy(
            src_ref=buf.at[k, slot], dst_ref=buf.at[k, slot],
            send_sem=part_s.at[k, d], recv_sem=part_r.at[k, d],
            device_id=partner, device_id_type=MESH,
        )

    def halo_copy(k, side):
        first = SHIFT_MAX if side == 0 else energies
        landing = SHIFT_MAX + energies if side == 0 else 0
        return pltpu.make_async_remote_copy(
            src_ref=buf.at[k, pl.ds(first, SHIFT_MAX)],
            dst_ref=buf.at[k, pl.ds(landing, SHIFT_MAX)],
            send_sem=halo_s.at[k, side], recv_sem=halo_r.at[k, side],
            device_id={"energy": e - 1 if side == 0 else e + 1}, device_id_type=MESH,
        )

    def ret_own_copy():
        return pltpu.make_async_copy(ret.at[0, pl.ds(2 * p, 2)], green.at[p], ret_own)

    def ret_copy(d, arriving=False):
        line = source(d) if arriving else p
        return pltpu.make_async_remote_copy(
            src_ref=ret.at[0, pl.ds(2 * peer(d), 2)], dst_ref=green.at[line],
            send_sem=ret_s.at[d], recv_sem=ret_r.at[d],
            device_id={"layer": 2 * peer(d) + q}, device_id_type=MESH,
        )

    def side_copies(arriving=False):
        at = 1 - q if arriving else q
        return (
            pltpu.make_async_remote_copy(
                src_ref=coupling.at[0], dst_ref=volt.at[at],
                send_sem=side_sem.at[0], recv_sem=side_sem.at[1],
                device_id=partner, device_id_type=MESH,
            ),
            pltpu.make_async_remote_copy(
                src_ref=alive.at[at], dst_ref=alive.at[at],
                send_sem=side_sem.at[2], recv_sem=side_sem.at[3],
                device_id=partner, device_id_type=MESH,
            ),
        )

    def side_own():
        return pltpu.make_async_copy(coupling.at[0], volt.at[q], side_sem.at[4])

    def chain_copy(c, i):
        return pltpu.make_async_remote_copy(
            src_ref=xout.at[c, 1, i], dst_ref=xin.at[c, i],
            send_sem=chain_s.at[c, i], recv_sem=chain_r.at[c, i],
            device_id={"layer": lax.rem(index + 2, 2 * lines)}, device_id_type=MESH,
        )

    def out_own(c, i):
        return pltpu.make_async_copy(
            xout.at[c, q, i], out.at[2 * i + q, 0, pl.ds(2 * c, 2)], out_sem.at[c, i]
        )

    def out_copy(c, i, arriving=False):
        parity = 1 - q if arriving else q
        return pltpu.make_async_remote_copy(
            src_ref=xout.at[c, 1 - q, i], dst_ref=out.at[2 * i + parity, 0, pl.ds(2 * c, 2)],
            send_sem=out_s.at[c, i], recv_sem=out_r.at[c, i],
            device_id=partner, device_id_type=MESH,
        )

    def start_line(k):
        own_copy(k).start()
        for d in range(1, lines):
            line_copy(k, d).start()

    def arrival(t):
        line = jnp.where(p < lines // 2, t, lines - 1 - t)
        return line, lax.rem(p + lines - line, lines)

    def pass_on(k):
        own_copy(k).wait()
        part_copy(k, 0).start()
        for t in range(lines):
            line, d = arrival(t)

            @pl.when(line != p)
            def _():
                line_copy(k, d, True).wait_recv()
                part_copy(k, d).start()

    def start_halo(k):
        for d in range(lines):
            part_copy(k, d, True).wait_recv()

        @pl.when(e > 0)
        def _():
            halo_copy(k, 0).start()

        @pl.when(e < groups - 1)
        def _():
            halo_copy(k, 1).start()

    def self_energy(k):
        c, a = divmod(k, 2)

        @pl.when(e < groups - 1)
        def _():
            halo_copy(k, 0).wait_recv()

        @pl.when(e > 0)
        def _():
            halo_copy(k, 1).wait_recv()

        absorb, emit = tap_weights(shifts, strengths)
        below, above = (absorb, emit) if c == 0 else (emit, absorb)
        count = alive[a, 0:1, :]
        column = lax.broadcasted_iota(jnp.int32, (ROWS, orbitals), 1)
        row = lax.broadcasted_iota(jnp.int32, (ROWS, orbitals), 0)
        tiles = orbitals // ROWS

        def one(step, carry):
            i = step // (2 * tiles)
            component = lax.rem(step // tiles, 2)
            base = pl.multiple_of(lax.rem(step, tiles) * ROWS, ROWS)
            here = slot_of(i, q)
            total = jnp.zeros((ROWS, orbitals), jnp.float32)
            for d in range(SHIFT_MAX):
                low = buf[k, here - d - 1, component, pl.ds(base, ROWS), :].astype(jnp.float32)
                high = buf[k, here + d + 1, component, pl.ds(base, ROWS), :].astype(jnp.float32)
                total = total + (below[d] * low + above[d] * high)
            keep = (row + base < count) & (column < count)
            sigma[k, i, component, pl.ds(base, ROWS), :] = jnp.where(keep, total, 0.0).astype(half)
            return carry

        lax.fori_loop(0, lines * 2 * tiles, one, 0)

    def advance(c, a, i, previous):
        k = 2 * c + a
        v = volt[a]
        g_real = green[i, a, 0]
        g_imag = green[i, a, 1]
        halfway = [dot_t(previous[n], v).astype(half) for n in range(2)]
        src = [
            (sigma[k, i, n].astype(jnp.float32) + dot(v, halfway[n])).astype(half) for n in range(2)
        ]
        inner_real = (dot(g_real, src[0]) - dot(g_imag, src[1])).astype(half)
        inner_imag = (dot(g_real, src[1]) + dot(g_imag, src[0])).astype(half)
        xout[c, a, i, 0] = (dot_t(inner_real, g_real) + dot_t(inner_imag, g_imag)).astype(half)
        xout[c, a, i, 1] = (dot_t(inner_imag, g_real) - dot_t(inner_real, g_imag)).astype(half)

    def sweep_energy(i, carry):
        @pl.when(i == p)
        def _():
            ret_own_copy().wait()

        @pl.when(i != p)
        def _():
            ret_copy(lax.rem(p + lines - i, lines), True).wait_recv()

        for c in range(2):
            @pl.when(p == 0)
            def _(c=c):
                xin[c, i] = buf[2 * c, slot_of(i, q)]

            @pl.when(p > 0)
            def _(c=c):
                chain_copy(c, i).wait_recv()

            advance(c, 0, i, xin.at[c, i])

            @pl.when(q == 1)
            def _(c=c):
                out_copy(c, i).start()

            advance(c, 1, i, xout.at[c, 0, i])

            @pl.when(q == 0)
            def _(c=c):
                out_copy(c, i).start()

            @pl.when(p < lines - 1)
            def _(c=c):
                if c == 1:
                    chain_copy(0, i).wait_send()
                else:
                    @pl.when(i > 0)
                    def _():
                        chain_copy(1, i - 1).wait_send()

                chain_copy(c, i).start()

            out_own(c, i).start()
        return carry

    start_line(0)
    alive[q] = jnp.full(alive.shape[1:], orbital_count[0], jnp.int32)
    start_line(1)
    side_own().start()
    for copy in side_copies():
        copy.start()

    for at, edge in ((0, 0), (SHIFT_MAX + energies, groups - 1)):
        @pl.when(e == edge)
        def _(at=at):
            def clear(step, carry):
                k = step // SHIFT_MAX
                slot = at + lax.rem(step, SHIFT_MAX)
                buf[k, slot] = jnp.zeros(buf.shape[2:], half)
                return carry

            lax.fori_loop(0, 4 * SHIFT_MAX, clear, 0)

    def start_ret():
        ret_own_copy().start()
        for d in range(1, lines):
            ret_copy(d).start()

    pass_on(0)
    start_line(2)
    pass_on(1)
    start_line(3)
    start_halo(0)
    pass_on(2)
    start_ret()
    start_halo(1)
    side_own().wait()
    for copy in side_copies(True):
        copy.wait_recv()
    self_energy(0)
    pass_on(3)
    start_halo(2)
    self_energy(1)
    start_halo(3)
    self_energy(2)
    self_energy(3)
    lax.fori_loop(0, lines, sweep_energy, 0)

    for copy in side_copies():
        copy.wait_send()
    for d in range(1, lines):
        ret_copy(d).wait_send()
        for k in range(4):
            line_copy(k, d).wait_send()
    for k in range(4):
        for d in range(lines):
            part_copy(k, d).wait_send()

        @pl.when(e > 0)
        def _(k=k):
            halo_copy(k, 0).wait_send()

        @pl.when(e < groups - 1)
        def _(k=k):
            halo_copy(k, 1).wait_send()

    @pl.when(p < lines - 1)
    def _():
        chain_copy(1, lines - 1).wait_send()

    for c in range(2):
        def finish(i, carry, c=c):
            out_own(c, i).wait()
            out_copy(c, i).wait_send()
            out_copy(c, i, True).wait_recv()
            return carry

        lax.fori_loop(0, lines, finish, 0)


def body(correlations, retarded, coupling, phonon_shifts, phonon_coupling, layer_orbitals):
    groups = lax.axis_size("energy")
    energies = lax.axis_size("layer")
    lines = energies // 2
    orbitals = correlations.shape[-1]
    block = (2, orbitals, orbitals)
    low = jnp.bfloat16
    shapes = [
        (4, energies + 2 * SHIFT_MAX) + block,
        (lines, 2) + block,
        (2, orbitals, orbitals),
        None,
        (4, lines) + block,
        (2, lines) + block,
        (2, 2, lines) + block,
    ]
    scratch = [
        pltpu.VMEM((2, 8, orbitals), jnp.int32) if shape is None else pltpu.VMEM(shape, low)
        for shape in shapes
    ]
    dma = pltpu.SemaphoreType.DMA
    semaphores = [
        dma((4,)), dma((4, lines)), dma((4, lines)), dma((4, lines)), dma((4, lines)),
        dma((4, 2)), dma((4, 2)),
        dma(()), dma((lines,)), dma((lines,)), dma((6,)),
        dma((2, lines)), dma((2, lines)), dma((2, lines)), dma((2, lines)), dma((2, lines)),
    ]
    large = pl.BlockSpec(memory_space=pltpu.HBM)
    anywhere = pl.BlockSpec(memory_space=pl.ANY)
    return pl.pallas_call(
        functools.partial(kernel, groups, lines, orbitals),
        out_shape=jax.ShapeDtypeStruct((energies, 1, 4, orbitals, orbitals), low),
        in_specs=[pl.BlockSpec(memory_space=pltpu.SMEM)] * 3 + [large] * 3,
        out_specs=anywhere,
        scratch_shapes=scratch + semaphores,
        compiler_params=pltpu.CompilerParams(
            collective_id=0, has_side_effects=True,
            vmem_limit_bytes=60 << 20,
        ),
        cost_estimate=pl.CostEstimate(
            flops=lines * 4 * 12 * 2 * orbitals**3, bytes_accessed=12 << 20, transcendentals=0
        ),
    )(phonon_shifts, phonon_coupling, layer_orbitals, correlations, retarded, coupling)


def solution(mesh):
    return jax.shard_map(
        body,
        mesh=mesh,
        in_specs=(
            P(("energy", "layer"), None, None, None, None),
            P(("energy", "layer"), None, None, None, None),
            P("layer", None, None),
            P(),
            P(),
            P("layer"),
        ),
        out_specs=P("energy", "layer", None, None, None),
        check_vma=False,
    )
```
